256 devices in a mesh: rows: 4 (over z_lo), cols: 64 (over z_hi, x, y, core).
Axes of the slice: x: 4, y: 4, z: 8 (z_hi: 2, z_lo: 4; z = z_hi * 4 + z_lo), core: 2. Of those that a mesh axis runs over, the one named last changes fastest.
Arguments:
- responses: bfloat16 [16384, 65536], P('rows', 'cols')
- test_matrix: bfloat16 [65536, 128], P('cols'), may hold values from -0.0234375 to 0.0234375
Outputs:
- refined_sketch: float32 [16384, 128], P(('rows', 'cols'))
The draws below stay inside these ranges and needn't reach their ends.
All inputs are finite; a program needn't handle non-finite values.
Results may differ from the reference program's by a relative error of at most 0.00165.
The reference program's roundings to bfloat16 on the way (of `left_basis` and `right_basis`) count: a program that leaves them out, or rounds other values in their place, can miss the bound.
Values may be sent and summed in bfloat16 or wider, within the bound.
A program may use at most 64 MiB of HBM per device.

```python
import math
import jax
import jax.numpy as jnp
from jax import lax

COLUMNS = 65536
SKETCH = 128
ROWS = 16384


def draw_responses(key, part):
    key = jax.random.fold_in(key, 11)
    base_key, row_key, col_key = jax.random.split(key, 3)
    position = jnp.arange(ROWS, dtype=jnp.float32) / (ROWS - 1)
    row_scale = jnp.exp(math.log(3.0) * position) * jnp.exp(jax.random.uniform(row_key, (ROWS,), jnp.float32, 0.0, math.log(3.0)))
    col_scale = jnp.exp(jax.random.uniform(col_key, (COLUMNS,), jnp.float32, 0.0, math.log(10.0)))
    base = jax.random.normal(base_key, (ROWS, COLUMNS), jnp.float32)
    return (0.05 * base * row_scale[:, None] * col_scale[None, :]).astype(jnp.bfloat16)


def levels(key, extent, cuts, least, top_value):
    def one(dim, shards_of):
        draws = jax.random.uniform(jax.random.fold_in(jax.random.fold_in(key, 6), dim), (shards_of,), jnp.float32, least / len(cuts), top_value / len(cuts))
        return jnp.repeat(jnp.exp(draws), extent[dim] // shards_of).reshape((-1,) + (1,) * (len(extent) - dim - 1))

    factor_of = one(*cuts[0])
    for cut in cuts[1:]:
        factor_of = factor_of * one(*cut)
    return factor_of


def gaussian(stream_key, shape, deviation, reach, shards=(), kind=jnp.bfloat16):
    drawn = jax.random.normal(stream_key, shape, jnp.float32) * deviation
    if len(shards) > 0:
        drawn = levels(stream_key, shape, shards, -0.22, 0.18) * drawn
    return jnp.clip(drawn, min=-reach, max=reach).astype(kind)


def setup_inputs(seed: int = 0) -> dict:
    key_list = jax.random.split(jax.random.key(seed), 3)
    responses = draw_responses(jax.random.fold_in(key_list[2], 71), 0)
    test_matrix = gaussian(key_list[1], (COLUMNS, SKETCH), COLUMNS ** -0.5, 0.0234375, ((0, 64),))
    return dict(responses=responses, test_matrix=test_matrix)


def orthonormal(panel):
    gram = jnp.dot(panel.T.astype(jnp.float32), panel.astype(jnp.float32), precision=lax.Precision.HIGHEST, preferred_element_type=jnp.float32)
    factor = jnp.linalg.cholesky(gram)
    basis = lax.linalg.triangular_solve(factor, panel, left_side=False, lower=True, transpose_a=True)
    return basis.astype(jnp.bfloat16)

def reference(responses, test_matrix):
    first_sketch = jnp.dot(responses.astype(jnp.float32), test_matrix.astype(jnp.float32), preferred_element_type=jnp.float32)
    left_basis = orthonormal(first_sketch)
    projected = lax.dot_general(responses.astype(jnp.float32), left_basis.astype(jnp.float32), (((0,), (0,)), ((), ())), preferred_element_type=jnp.float32)
    right_basis = orthonormal(projected)
    return jnp.dot(responses.astype(jnp.float32), right_basis.astype(jnp.float32), preferred_element_type=jnp.float32)
```

```python
import functools

import jax
import jax.numpy as jnp
from jax import lax
from jax.experimental import pallas as pl
from jax.experimental.pallas import tpu as pltpu
from jax.sharding import PartitionSpec as P

F32 = jnp.float32
BF16 = jnp.bfloat16
MESH = pl.DeviceIdType.MESH
HIGH = lax.Precision.HIGHEST

PLANE = sorted(
    [(i, j) for i in range(4) for j in range(4) if i or j],
    key=lambda o: -(min(o[0], 4 - o[0]) + min(o[1], 4 - o[1])),
)


def inverse_factor(gram):
    lane = lax.broadcasted_iota(jnp.int32, (8, 128), 1)
    sub = lax.broadcasted_iota(jnp.int32, (8, 128), 0)
    lane1 = lane[:1]
    rows = [gram[8 * i : 8 * i + 8] for i in range(16)]
    for kb in range(16):
        o = 8 * kb
        head = rows[kb]
        col = [jnp.broadcast_to(head[:, o + j : o + j + 1], (8, 128)) for j in range(8)]
        inverses, pivots, above = [], [], {}
        for r in range(8):
            inv = 1.0 / col[r][r : r + 1]
            inverses.append(inv)
            for j in range(r + 1, 8):
                above[r, j] = col[j][r : r + 1]
            q = jnp.where(lane1 == o + r, 1.0, head[r : r + 1]) * inv
            pivots.append(jnp.where((lane1 > o + r) & (lane1 < o + 8), 0.0, q))
            if r < 7:
                c = jnp.where(sub > r, col[r], 0.0)
                f = c * inv
                for j in range(r + 1, 8):
                    col[j] = col[j] - f * above[r, j]
                head = jnp.where((lane == o + r) & (sub > r), 0.0, head) - c * q
        rows[kb] = head
        inside = (lane >= o) & (lane < o + 8)
        for i in range(kb + 1, 16):
            c = [jnp.broadcast_to(rows[i][:, o + j : o + j + 1], (8, 128)) for j in range(8)]
            x = jnp.where(inside, 0.0, rows[i])
            for r in range(8):
                f = c[r] * inverses[r]
                for j in range(r + 1, 8):
                    c[j] = c[j] - f * above[r, j]
                x = x - c[r] * pivots[r]
            rows[i] = x
    full = jnp.concatenate(rows, axis=0)
    r = lax.broadcasted_iota(jnp.int32, (128, 128), 0)
    c = lax.broadcasted_iota(jnp.int32, (128, 128), 1)
    d = jnp.sum(jnp.where(r == c, full, 0.0), axis=1, keepdims=True)
    return jnp.where(r > c, full, jnp.where(r == c, 1.0, 0.0)) * lax.rsqrt(d)


def kernel(
    a_hbm, t_hbm, out_ref,
    a, t, part1, core1, plane1, hi1, sketch, left, proj, projx, projf, right,
    part3, core3, plane3, hi3,
    gram1, gx1, gs1, full1, gram2, gx2, gs2, full2,
    load_sem, s_core1, r_core1, s_plane1, r_plane1, s_hi1, r_hi1,
    s_core3, r_core3, s_plane3, r_plane3, s_hi3, r_hi3,
    s_g1, r_g1, s_z1, r_z1, s_b1, r_b1,
    s_g2, r_g2, s_z2, r_z2, s_b2, r_b2,
    s_ag, r_ag, s_fw, r_fw, s_p, r_p, s_pf, r_pf,
):
    zl = lax.axis_index("rows")
    ci = lax.axis_index("cols")
    zh, x, y, k = ci // 32, (ci // 8) % 4, (ci // 2) % 4, ci % 2

    def at(zl_, zh_, x_, y_, k_):
        return (zl_, ((zh_ * 4 + x_) * 4 + y_) * 2 + k_)

    other_core = at(zl, zh, x, y, 1 - k)
    other_hi = at(zl, 1 - zh, x, y, k)

    def plane_peer(o):
        return (x + o[0]) % 4, (y + o[1]) % 4

    def plane_dev(o):
        px, py = plane_peer(o)
        return at(zl, zh, px, py, k)

    def remote(src, dst, ss, rs, dev):
        return pltpu.make_async_remote_copy(
            src_ref=src, dst_ref=dst, send_sem=ss, recv_sem=rs, device_id=dev, device_id_type=MESH
        )

    column = [(dz, dk) for dz in (4, 3, 5, 2, 6, 1, 7, 0) for dk in (0, 1) if dz or dk]
    nearby = [(dz, dk) for dz in (2, 3, 1, 0) for dk in (0, 1) if dz or dk]

    def column_dev(dz, dk):
        z = (zh * 4 + zl + dz) % 8
        return at(z % 4, z // 4, x, y, (k + dk) % 2)

    def nearby_dev(dz, dk):
        return at((zl + dz) % 4, zh, x, y, (k + dk) % 2)

    load_t = pltpu.make_async_copy(t_hbm, t, load_sem.at[8])
    load_t.start()
    loads = []
    order = (2, 1, 3, 0)
    for n, dx in enumerate(order):
        px = (x + dx) % 4
        for h in range(2):
            ref = pl.ds(pl.multiple_of(h * 2048 + px * 512, 512), 512)
            copy = pltpu.make_async_copy(a_hbm.at[ref, :], a.at[ref, :], load_sem.at[2 * n + h])
            copy.start()
            loads.append(copy)

    barrier = pltpu.get_barrier_semaphore()
    for o in PLANE:
        pl.semaphore_signal(barrier, inc=1, device_id=plane_dev(o), device_id_type=MESH)
    for dz, dk in column:
        pl.semaphore_signal(barrier, inc=1, device_id=column_dev(dz, dk), device_id_type=MESH)

    def reduce_columns(weights, part, core, plane, s_core, r_core, s_plane, r_plane, first):
        sends = []

        def add_and_send(dx):
            px = (x + dx) % 4
            cores[dx].wait_recv()
            for py in range(4):
                part[:, px, py, k] = part[:, px, py, k] + core[px, :, py]
            for s, o in enumerate(PLANE):
                if o[0] != dx:
                    continue
                _, py = plane_peer(o)
                copy = remote(part.at[:, px, py, k], plane.at[s], s_plane.at[s], r_plane.at[s], plane_dev(o))
                copy.start()
                sends.append(copy)

        cores = {}
        for n, dx in enumerate(order):
            px = (x + dx) % 4
            for h in range(2):
                if first:
                    loads[2 * n + h].wait()
                ref = pl.ds(pl.multiple_of(h * 2048 + px * 512, 512), 512)
                piece = jnp.dot(a[ref, :], weights[...], preferred_element_type=F32)
                part[h, px] = piece.reshape(4, 2, 64, 128)
            if first and n == 0:
                pl.semaphore_wait(barrier, len(PLANE) + len(column))
            cores[dx] = remote(
                part.at[:, px, :, 1 - k], core.at[px], s_core.at[n], r_core.at[n], other_core
            )
            cores[dx].start()
            if n:
                add_and_send(order[n - 1])
        add_and_send(order[-1])
        total = part[:, x, y, k]
        for s in range(15):
            remote(plane.at[s], plane.at[s], s_plane.at[s], r_plane.at[s], other_core).wait_recv()
            total = total + plane[s]
        return total, list(cores.values()) + sends

    def all_reduce(gram, gx, gs, full, s_g, r_g, s_z, r_z, s_b, r_b, group, group_dev, group_slot):
        sends = []
        mine = x * 4 + y
        for s, o in enumerate(PLANE):
            px, py = plane_peer(o)
            copy = remote(gram.at[px * 4 + py], gx.at[s], s_g.at[s], r_g.at[s], plane_dev(o))
            copy.start()
            sends.append(copy)
        yield
        total = gram[mine]
        for s in range(15):
            sends[s].wait_recv()
            total = total + gx[s]
        slot = group_slot(0, 0)
        gs[slot] = total
        for s, o in enumerate(group):
            copy = remote(gs.at[slot], gs.at[slot], s_z.at[s], r_z.at[s], group_dev(*o))
            copy.start()
            sends.append(copy)
        for copy in sends[15:]:
            copy.wait_recv()
        total = gs[0]
        for s in range(1, len(group) + 1):
            total = total + gs[s]
        full[mine] = total
        casts = []
        for s, o in enumerate(PLANE):
            copy = remote(full.at[mine], full.at[mine], s_b.at[s], r_b.at[s], plane_dev(o))
            copy.start()
            casts.append(copy)
        for copy in casts:
            copy.wait_recv()
        for copy in sends + casts:
            copy.wait_send()
        yield

    load_t.wait()
    total, pending1 = reduce_columns(
        t, part1, core1, plane1, s_core1, r_core1, s_plane1, r_plane1, True
    )
    hi1[0] = total
    swap = remote(hi1.at[0], hi1.at[1], s_hi1, r_hi1, other_hi)
    swap.start()
    swap.wait_recv()
    total = total + hi1[1]
    sketch[:, x, y, k] = total
    rows = total.reshape(128, 128)
    gram1[...] = lax.dot_general(
        rows, rows, (((0,), (0,)), ((), ())), precision=HIGH, preferred_element_type=F32
    ).reshape(16, 8, 128)
    reduction = all_reduce(
        gram1, gx1, gs1, full1, s_g1, r_g1, s_z1, r_z1, s_b1, r_b1, nearby, nearby_dev,
        lambda dz, dk: ((zl + dz) % 4) * 2 + (k + dk) % 2,
    )
    next(reduction)
    spread = []
    for s, o in enumerate(PLANE):
        mine = sketch.at[:, x, y, k]
        copy = remote(mine, mine, s_ag.at[s], r_ag.at[s], plane_dev(o))
        copy.start()
        spread.append(copy)
    next(reduction)
    forward = []
    for n in range(4):
        for s, o in enumerate(PLANE):
            if (4 - o[0]) % 4 == n:
                spread[s].wait_recv()
        mine = sketch.at[:, (x + n) % 4, :, k]
        copy = remote(mine, mine, s_fw.at[n], r_fw.at[n], other_core)
        copy.start()
        forward.append(copy)
    factor = inverse_factor(full1[...].reshape(128, 128))
    for copy in forward:
        copy.wait_recv()

    for h in range(2):
        for px in range(4):
            piece = lax.dot_general(
                factor, sketch[h, px].reshape(512, 128), (((1,), (1,)), ((), ())),
                precision=HIGH, preferred_element_type=F32,
            )
            left[:, h * 2048 + px * 512 : h * 2048 + px * 512 + 512] = piece.astype(BF16)

    gives = []
    for n, dz in enumerate((2, 1, 3, 0)):
        pz = (zl + dz) % 4
        ref = pl.ds(pl.multiple_of(pz * 256, 256), 256)
        proj[pz] = jnp.dot(left[...], a[:, ref], preferred_element_type=F32)
        if dz:
            copy = remote(proj.at[pz], projx.at[n], s_p.at[n], r_p.at[n], at(pz, zh, x, y, k))
            copy.start()
            gives.append(copy)
    total = proj[zl]
    for n in range(3):
        gives[n].wait_recv()
        total = total + projx[n]
    projf[zl] = total
    gram2[...] = lax.dot_general(
        total, total, (((1,), (1,)), ((), ())), precision=HIGH, preferred_element_type=F32
    ).reshape(16, 8, 128)
    reduction = all_reduce(
        gram2, gx2, gs2, full2, s_g2, r_g2, s_z2, r_z2, s_b2, r_b2, column, column_dev,
        lambda dz, dk: ((zh * 4 + zl + dz) % 8) * 2 + (k + dk) % 2,
    )
    next(reduction)
    shares = []
    for n, dz in enumerate((2, 1, 3)):
        copy = remote(
            projf.at[zl], projf.at[zl], s_pf.at[n], r_pf.at[n], at((zl + dz) % 4, zh, x, y, k)
        )
        copy.start()
        shares.append(copy)
    next(reduction)
    factor = inverse_factor(full2[...].reshape(128, 128))
    for copy in shares:
        copy.wait_recv()

    for pz in range(4):
        piece = jnp.dot(factor, projf[pz], precision=HIGH, preferred_element_type=F32)
        right[pz * 256 : pz * 256 + 256, :] = piece.T.astype(BF16)

    total, pending3 = reduce_columns(
        right, part3, core3, plane3, s_core3, r_core3, s_plane3, r_plane3, False
    )
    hi3[0] = total
    swap3 = remote(hi3.at[0, 1 - zh], hi3.at[1, 0], s_hi3, r_hi3, other_hi)
    swap3.start()
    swap3.wait_recv()
    out_ref[...] = hi3[0, zh] + hi3[1, 0]
    for copy in pending1 + [swap] + spread + forward + gives + shares + pending3 + [swap3]:
        copy.wait_send()


def local(responses, test_matrix):
    v = pltpu.VMEM
    dma = pltpu.SemaphoreType.DMA
    scratch = [
        v((4096, 1024), BF16), v((1024, 128), BF16),
        v((2, 4, 4, 2, 64, 128), F32), v((4, 2, 4, 64, 128), F32), v((15, 2, 64, 128), F32), v((2, 2, 64, 128), F32),
        v((2, 4, 4, 2, 64, 128), F32), v((128, 4096), BF16),
        v((4, 128, 256), F32), v((3, 128, 256), F32), v((4, 128, 256), F32), v((1024, 128), BF16),
        v((2, 4, 4, 2, 64, 128), F32), v((4, 2, 4, 64, 128), F32), v((15, 2, 64, 128), F32), v((2, 2, 64, 128), F32),
        v((16, 8, 128), F32), v((15, 8, 128), F32), v((8, 8, 128), F32), v((16, 8, 128), F32),
        v((16, 8, 128), F32), v((15, 8, 128), F32), v((16, 8, 128), F32), v((16, 8, 128), F32),
        dma((9,)),
    ]
    scratch += [dma((4,)), dma((4,)), dma((15,)), dma((15,)), dma, dma] * 2
    scratch += [dma((15,)), dma((15,)), dma((7,)), dma((7,)), dma((15,)), dma((15,))]
    scratch += [dma((15,)), dma((15,)), dma((15,)), dma((15,)), dma((15,)), dma((15,))]
    scratch += [dma((15,)), dma((15,)), dma((4,)), dma((4,)), dma((3,)), dma((3,)), dma((3,)), dma((3,))]
    return pl.pallas_call(
        kernel,
        out_shape=jax.ShapeDtypeStruct((64, 128), F32),
        in_specs=[pl.BlockSpec(memory_space=pl.ANY)] * 2,
        out_specs=pl.BlockSpec(memory_space=pltpu.VMEM),
        scratch_shapes=scratch,
        compiler_params=pltpu.CompilerParams(
            collective_id=0, has_side_effects=True, vmem_limit_bytes=48 * 2**20
        ),
        name="power_iteration",
    )(responses, test_matrix)


def solution(mesh):
    in_specs = (P("rows", "cols"), P("cols", None))
    out_specs = P(("rows", "cols"), None)
    return jax.shard_map(local, mesh=mesh, in_specs=in_specs, out_specs=out_specs, check_vma=False)
```

```python
import functools

import jax
import jax.numpy as jnp
from jax import lax
from jax.experimental import pallas as pl
from jax.experimental.pallas import tpu as pltpu
from jax.sharding import PartitionSpec as P

F32 = jnp.float32
BF16 = jnp.bfloat16
MESH = pl.DeviceIdType.MESH
HIGH = lax.Precision.HIGHEST

PLANE = sorted(
    [(i, j) for i in range(4) for j in range(4) if i or j],
    key=lambda o: -(min(o[0], 4 - o[0]) + min(o[1], 4 - o[1])),
)


def inverse_factor(gram):
    lane = lax.broadcasted_iota(jnp.int32, (8, 128), 1)
    sub = lax.broadcasted_iota(jnp.int32, (8, 128), 0)
    lane1 = lane[:1]
    rows = [gram[8 * i : 8 * i + 8] for i in range(16)]
    for kb in range(16):
        o = 8 * kb
        head = rows[kb]
        col = [jnp.broadcast_to(head[:, o + j : o + j + 1], (8, 128)) for j in range(8)]
        inverses, pivots, above = [], [], {}
        for r in range(8):
            inv = 1.0 / col[r][r : r + 1]
            inverses.append(inv)
            for j in range(r + 1, 8):
                above[r, j] = col[j][r : r + 1]
            q = jnp.where(lane1 == o + r, 1.0, head[r : r + 1]) * inv
            pivots.append(jnp.where((lane1 > o + r) & (lane1 < o + 8), 0.0, q))
            if r < 7:
                c = jnp.where(sub > r, col[r], 0.0)
                f = c * inv
                for j in range(r + 1, 8):
                    col[j] = col[j] - f * above[r, j]
                head = jnp.where((lane == o + r) & (sub > r), 0.0, head) - c * q
        rows[kb] = head
        inside = (lane >= o) & (lane < o + 8)
        for i in range(kb + 1, 16):
            c = [jnp.broadcast_to(rows[i][:, o + j : o + j + 1], (8, 128)) for j in range(8)]
            x = jnp.where(inside, 0.0, rows[i])
            for r in range(8):
                f = c[r] * inverses[r]
                for j in range(r + 1, 8):
                    c[j] = c[j] - f * above[r, j]
                x = x - c[r] * pivots[r]
            rows[i] = x
    full = jnp.concatenate(rows, axis=0)
    r = lax.broadcasted_iota(jnp.int32, (128, 128), 0)
    c = lax.broadcasted_iota(jnp.int32, (128, 128), 1)
    d = jnp.sum(jnp.where(r == c, full, 0.0), axis=1, keepdims=True)
    return jnp.where(r > c, full, jnp.where(r == c, 1.0, 0.0)) * lax.rsqrt(d)


def kernel(
    a_hbm, t_hbm, out_ref,
    a, t, part1, core1, got1, acc1, last1, hi1, sketch, left, proj, projx, projf, right,
    part3, core3, got3, acc3, last3, hi3,
    grams, stack1, full1, gram2, gx2, gs2, full2, factor1, factor2,
    load_sem, s_core1, r_core1, s_one1, r_one1, s_two1, r_two1, s_hi1, r_hi1,
    s_core3, r_core3, s_one3, r_one3, s_two3, r_two3, s_hi3, r_hi3,
    s_g1, r_g1, s_z1, r_z1,
    s_g2, r_g2, s_z2, r_z2, s_b2, r_b2,
    s_ag, r_ag, s_fw, r_fw, s_p, r_p, s_pf, r_pf,
):
    zl = lax.axis_index("rows")
    ci = lax.axis_index("cols")
    zh, x, y, k = ci // 32, (ci // 8) % 4, (ci // 2) % 4, ci % 2

    def block(body):
        pl.when(zl >= 0)(body)

    def at(zl_, zh_, x_, y_, k_):
        return (zl_, ((zh_ * 4 + x_) * 4 + y_) * 2 + k_)

    other_core = at(zl, zh, x, y, 1 - k)
    other_hi = at(zl, 1 - zh, x, y, k)

    def plane_peer(o):
        return (x + o[0]) % 4, (y + o[1]) % 4

    def plane_dev(o):
        px, py = plane_peer(o)
        return at(zl, zh, px, py, k)

    def remote(src, dst, ss, rs, dev):
        return pltpu.make_async_remote_copy(
            src_ref=src, dst_ref=dst, send_sem=ss, recv_sem=rs, device_id=dev, device_id_type=MESH
        )

    column = [(dz, dk) for dz in (4, 3, 5, 2, 6, 1, 7, 0) for dk in (0, 1) if dz or dk]

    def column_dev(dz, dk):
        z = (zh * 4 + zl + dz) % 8
        return at(z % 4, z // 4, x, y, (k + dk) % 2)

    load_t = pltpu.make_async_copy(t_hbm, t, load_sem.at[8])
    load_t.start()
    loads = []
    order = (2, 1, 3, 0)
    for n, dx in enumerate(order):
        px = (x + dx) % 4
        for h in range(2):
            ref = pl.ds(pl.multiple_of(h * 2048 + px * 512, 512), 512)
            copy = pltpu.make_async_copy(a_hbm.at[ref, :], a.at[ref, :], load_sem.at[2 * n + h])
            copy.start()
            loads.append(copy)

    barrier = pltpu.get_barrier_semaphore()
    for o in PLANE:
        pl.semaphore_signal(barrier, inc=1, device_id=plane_dev(o), device_id_type=MESH)
    for dz, dk in column:
        pl.semaphore_signal(barrier, inc=1, device_id=column_dev(dz, dk), device_id_type=MESH)

    def x_dev(d):
        return at(zl, zh, (x + d) % 4, y, k)

    def y_dev(d):
        return at(zl, zh, x, (y + d) % 4, k)

    top, low = pl.ds(0, 32), pl.ds(32, 32)
    around = (2, 1, 3)

    def reduce_columns(weights, part, core, got, acc, last, s_core, r_core, s_one, r_one, s_two, r_two, first, after):
        cores, ones = {}, []

        def exchange(n, dx):
            px = (x + dx) % 4
            cores[dx] = remote(
                part.at[:, px, :, 1 - k], core.at[px], s_core.at[n], r_core.at[n], other_core
            )
            cores[dx].start()

        def add_and_send(dx):
            px = (x + dx) % 4
            cores[dx].wait_recv()
            for py in range(4):
                part[:, px, py, k] = part[:, px, py, k] + core[px, :, py]
            if dx:
                copy = remote(
                    part.at[:, px, :, k, top], got.at[0, dx - 1], s_one.at[0, dx - 1], r_one.at[0, dx - 1], x_dev(dx)
                )
                copy.start()
                ones.append(copy)
            for d in around:
                remote(
                    part.at[:, px, (y + d) % 4, k, low], got.at[1, d - 1, :, px], s_one.at[1, d - 1],
                    r_one.at[1, d - 1], y_dev(d),
                ).start()

        for n, dx in enumerate(order):
            px = (x + dx) % 4
            for h in range(2):
                if first:
                    loads[2 * n + h].wait()

                @block
                def _(h=h, px=px):
                    ref = pl.ds(pl.multiple_of(h * 2048 + px * 512, 512), 512)
                    piece = jnp.dot(a[ref, :], weights[...], preferred_element_type=F32)
                    part[h, px] = piece.reshape(4, 2, 64, 128)

            if not first:
                exchange(n, dx)
                after(n)
                if n:
                    add_and_send(order[n - 1])
        if first:
            pl.semaphore_wait(barrier, len(PLANE) + len(column))
            for n, dx in enumerate(order):
                exchange(n, dx)
            for dx in order[:-1]:
                add_and_send(dx)
        add_and_send(order[-1])
        after(4)
        for d in around:
            ones.append(
                remote(
                    part.at[:, :, (y + d) % 4, k, low], got.at[1, d - 1], s_one.at[1, d - 1], r_one.at[1, d - 1], y_dev(d)
                )
            )
        for copy in ones[:3]:
            copy.wait_recv()
        for i in range(4):
            acc[0, i] = part[:, x, i, k, top] + (got[0, 0, :, i] + got[0, 1, :, i]) + got[0, 2, :, i]
        twos = []
        for d in around:
            copy = remote(
                acc.at[0, (y + d) % 4], last.at[0, d - 1], s_two.at[0, d - 1], r_two.at[0, d - 1], y_dev(d)
            )
            copy.start()
            twos.append(copy)
        for copy in ones[3:]:
            copy.wait_recv()
        for i in range(4):
            acc[1, i] = part[:, i, y, k, low] + (got[1, 0, :, i] + got[1, 1, :, i]) + got[1, 2, :, i]
        for d in around:
            copy = remote(
                acc.at[1, (x + d) % 4], last.at[1, d - 1], s_two.at[1, d - 1], r_two.at[1, d - 1], x_dev(d)
            )
            copy.start()
            twos.append(copy)
        for copy in twos:
            copy.wait_recv()
        return (
            acc[0, y] + (last[0, 0] + last[0, 1]) + last[0, 2],
            acc[1, x] + (last[1, 0] + last[1, 1]) + last[1, 2],
            list(cores.values()) + ones + twos,
        )

    def all_reduce(gram, gx, gs, full, s_g, r_g, s_z, r_z, s_b, r_b, group, group_dev, group_slot):
        sends = []
        mine = x * 4 + y
        for s, o in enumerate(PLANE):
            px, py = plane_peer(o)
            copy = remote(gram.at[px * 4 + py], gx.at[s], s_g.at[s], r_g.at[s], plane_dev(o))
            copy.start()
            sends.append(copy)
        yield
        total = gram[mine]
        for s in range(15):
            sends[s].wait_recv()
            total = total + gx[s]
        slot = group_slot(0, 0)
        gs[slot] = total
        for s, o in enumerate(group):
            copy = remote(gs.at[slot], gs.at[slot], s_z.at[s], r_z.at[s], group_dev(*o))
            copy.start()
            sends.append(copy)
        yield
        for copy in sends[15:]:
            copy.wait_recv()
        total = gs[0]
        for s in range(1, len(group) + 1):
            total = total + gs[s]
        full[mine] = total
        casts = []
        for s, o in enumerate(PLANE):
            copy = remote(full.at[mine], full.at[mine], s_b.at[s], r_b.at[s], plane_dev(o))
            copy.start()
            casts.append(copy)
        yield
        for copy in casts:
            copy.wait_recv()
        for copy in sends + casts:
            copy.wait_send()
        yield

    load_t.wait()
    upper, lower, pending1 = reduce_columns(
        t, part1, core1, got1, acc1, last1, s_core1, r_core1, s_one1, r_one1, s_two1, r_two1, True, lambda n: None
    )
    hi1[0, :, top] = upper
    hi1[0, :, low] = lower
    swap = remote(hi1.at[0], hi1.at[1], s_hi1, r_hi1, other_hi)
    swap.start()
    swap.wait_recv()
    sketch[:, x, y, k] = hi1[0] + hi1[1]

    spread = [[], []]
    for half, rows, devs in ((0, top, y_dev), (1, low, x_dev)):
        for d in around:
            mine = sketch.at[:, x, y, k, rows]
            copy = remote(mine, mine, s_ag.at[half, 0, d - 1], r_ag.at[half, 0, d - 1], devs(d))
            copy.start()
            spread[half].append(copy)
    forward = {}

    def strip(half, d):
        if half:
            return sketch.at[:, :, (y + d) % 4, k, low]
        return sketch.at[:, (x + d) % 4, :, k, top]

    def to_core(half, d):
        forward[half, d] = remote(
            strip(half, d), strip(half, d), s_fw.at[half, d], r_fw.at[half, d], other_core
        )
        forward[half, d].start()

    for half, devs in ((0, x_dev), (1, y_dev)):
        for copy in spread[half]:
            copy.wait_recv()
        for d in around:
            mine = strip(half, 0)
            copy = remote(mine, mine, s_ag.at[half, 1, d - 1], r_ag.at[half, 1, d - 1], devs(d))
            copy.start()
            spread[half].append(copy)
        to_core(half, 0)

    def gram_of(half, d):
        forward[half, d].wait_recv()

        @block
        def _():
            if half:
                p = (y + d) % 4
                rows = sketch[:, :, p, :, low].reshape(512, 128)
            else:
                p = (x + d) % 4
                rows = sketch[:, p, :, :, top].reshape(512, 128)
            grams[half, p] = lax.dot_general(
                rows, rows, (((0,), (0,)), ((), ())), precision=HIGH, preferred_element_type=F32
            )

    before = 0
    for d in (1, 3, 2):
        for half in range(2):
            spread[half][3 + around.index(d)].wait_recv()
            to_core(half, (4 - d) % 4)
        for half in range(2):
            gram_of(half, before)
        before = (4 - d) % 4
    for half in range(2):
        gram_of(half, before)
    mid = pl.ds(pl.multiple_of(k * 64, 64), 64)
    sums = [grams[h, 0, mid] + grams[h, 1, mid] + (grams[h, 2, mid] + grams[h, 3, mid]) for h in range(2)]
    stack1[zl] = sums[0] + sums[1]
    stacks = []
    for n, dz in enumerate((2, 3, 1)):
        copy = remote(stack1.at[zl], stack1.at[zl], s_z1.at[n], r_z1.at[n], at((zl + dz) % 4, zh, x, y, k))
        copy.start()
        stacks.append(copy)
    for copy in stacks:
        copy.wait_recv()
    full1[k] = (stack1[0] + stack1[1]) + (stack1[2] + stack1[3])
    halves = remote(full1.at[k], full1.at[k], s_g1, r_g1, other_core)
    halves.start()
    halves.wait_recv()

    @block
    def _():
        factor1[...] = inverse_factor(full1[...].reshape(128, 128))

    gram = full1[...].reshape(128, 128)
    diag = lax.broadcasted_iota(jnp.int32, (128, 128), 0) == lax.broadcasted_iota(jnp.int32, (128, 128), 1)
    scale = lax.rsqrt(jnp.sum(jnp.where(diag, gram, 0.0), keepdims=True) / 128)

    for h in range(2):
        for px in range(4):
            piece = lax.dot_general(
                factor1[...], sketch[h, px].reshape(512, 128), (((1,), (1,)), ((), ())),
                precision=HIGH, preferred_element_type=F32,
            )
            left[:, h * 2048 + px * 512 : h * 2048 + px * 512 + 512] = piece.astype(BF16)

    gives = []
    for n, dz in enumerate((2, 1, 3, 0)):
        pz = (zl + dz) % 4

        @block
        def _(pz=pz):
            ref = pl.ds(pl.multiple_of(pz * 256, 256), 256)
            proj[pz] = jnp.dot(left[...], a[:, ref], preferred_element_type=F32)

        if dz:
            copy = remote(proj.at[pz], projx.at[n], s_p.at[n], r_p.at[n], at(pz, zh, x, y, k))
            copy.start()
            gives.append(copy)
    total = proj[zl]
    for n in range(3):
        gives[n].wait_recv()
        total = total + projx[n]
    total = total * scale
    projf[zl] = total.astype(BF16)
    shares = []
    for n, dz in enumerate((2, 1, 3)):
        copy = remote(
            projf.at[zl], projf.at[zl], s_pf.at[n], r_pf.at[n], at((zl + dz) % 4, zh, x, y, k)
        )
        copy.start()
        shares.append(copy)
    gram2[...] = lax.dot_general(
        total, total, (((1,), (1,)), ((), ())), precision=HIGH, preferred_element_type=F32
    ).reshape(16, 8, 128)
    reduction = all_reduce(
        gram2, gx2, gs2, full2, s_g2, r_g2, s_z2, r_z2, s_b2, r_b2, column, column_dev,
        lambda dz, dk: ((zh * 4 + zl + dz) % 8) * 2 + (k + dk) % 2,
    )
    next(reduction)
    for copy in shares:
        copy.wait_recv()

    for pz in range(4):
        right[pz * 256 : pz * 256 + 256, :] = projf[pz].T

    def step(n):
        if n in (0, 4):
            next(reduction)

    upper, lower, pending3 = reduce_columns(
        right, part3, core3, got3, acc3, last3, s_core3, r_core3, s_one3, r_one3, s_two3, r_two3, False, step
    )
    hi3[0, :, top] = upper
    hi3[0, :, low] = lower
    swap3 = remote(hi3.at[0, 1 - zh], hi3.at[1, 0], s_hi3, r_hi3, other_hi)
    swap3.start()
    next(reduction)

    @block
    def _():
        factor2[...] = inverse_factor(full2[...].reshape(128, 128))

    swap3.wait_recv()
    out_ref[...] = lax.dot_general(
        hi3[0, zh] + hi3[1, 0], factor2[...], (((1,), (1,)), ((), ())),
        precision=HIGH, preferred_element_type=F32,
    )
    for copy in pending1 + [swap, halves] + spread[0] + spread[1] + list(forward.values()) + stacks + gives + shares + pending3 + [swap3]:
        copy.wait_send()


def local(responses, test_matrix):
    v = pltpu.VMEM
    dma = pltpu.SemaphoreType.DMA
    scratch = [
        v((4096, 1024), BF16), v((1024, 128), BF16),
        v((2, 4, 4, 2, 64, 128), F32), v((4, 2, 4, 64, 128), F32), v((2, 3, 2, 4, 32, 128), F32), v((2, 4, 2, 32, 128), F32), v((2, 3, 2, 32, 128), F32), v((2, 2, 64, 128), F32),
        v((2, 4, 4, 2, 64, 128), F32), v((128, 4096), BF16),
        v((4, 128, 256), F32), v((3, 128, 256), F32), v((4, 128, 256), BF16), v((1024, 128), BF16),
        v((2, 4, 4, 2, 64, 128), F32), v((4, 2, 4, 64, 128), F32), v((2, 3, 2, 4, 32, 128), F32), v((2, 4, 2, 32, 128), F32), v((2, 3, 2, 32, 128), F32), v((2, 2, 64, 128), F32),
        v((2, 4, 128, 128), F32), v((4, 64, 128), F32), v((2, 64, 128), F32),
        v((16, 8, 128), F32), v((15, 8, 128), F32), v((16, 8, 128), F32), v((16, 8, 128), F32),
        v((128, 128), F32), v((128, 128), F32),
        dma((9,)),
    ]
    scratch += [dma((4,)), dma((4,)), dma((2, 3)), dma((2, 3)), dma((2, 3)), dma((2, 3)), dma, dma] * 2
    scratch += [dma, dma, dma((3,)), dma((3,))]
    scratch += [dma((15,)), dma((15,)), dma((15,)), dma((15,)), dma((15,)), dma((15,))]
    scratch += [dma((2, 2, 3)), dma((2, 2, 3)), dma((2, 4)), dma((2, 4)), dma((3,)), dma((3,)), dma((3,)), dma((3,))]
    return pl.pallas_call(
        kernel,
        out_shape=jax.ShapeDtypeStruct((64, 128), F32),
        in_specs=[pl.BlockSpec(memory_space=pltpu.HBM)] * 2,
        out_specs=pl.BlockSpec(memory_space=pltpu.VMEM),
        scratch_shapes=scratch,
        compiler_params=pltpu.CompilerParams(
            collective_id=0, has_side_effects=True, vmem_limit_bytes=64 * 2**20 - 2**17
        ),
        name="power_iteration",
    )(responses, test_matrix)


def solution(mesh):
    in_specs = (P("rows", "cols"), P("cols", None))
    out_specs = P(("rows", "cols"), None)
    return jax.shard_map(local, mesh=mesh, in_specs=in_specs, out_specs=out_specs, check_vma=False)
```

```python
import functools

import jax
import jax.numpy as jnp
from jax import lax
from jax.experimental import pallas as pl
from jax.experimental.pallas import tpu as pltpu
from jax.sharding import PartitionSpec as P

F32 = jnp.float32
BF16 = jnp.bfloat16
MESH = pl.DeviceIdType.MESH
HIGH = lax.Precision.HIGHEST

PLANE = sorted(
    [(i, j) for i in range(4) for j in range(4) if i or j],
    key=lambda o: -(min(o[0], 4 - o[0]) + min(o[1], 4 - o[1])),
)


def inverse_factor(gram):
    lane = lax.broadcasted_iota(jnp.int32, (8, 128), 1)
    sub = lax.broadcasted_iota(jnp.int32, (8, 128), 0)
    lane1 = lane[:1]
    rows = [gram[8 * i : 8 * i + 8] for i in range(16)]
    for kb in range(16):
        o = 8 * kb
        head = rows[kb]
        col = [jnp.broadcast_to(head[:, o + j : o + j + 1], (8, 128)) for j in range(8)]
        inverses, pivots, above = [], [], {}
        for r in range(8):
            inv = 1.0 / col[r][r : r + 1]
            inverses.append(inv)
            for j in range(r + 1, 8):
                above[r, j] = col[j][r : r + 1]
            q = jnp.where(lane1 == o + r, 1.0, head[r : r + 1]) * inv
            pivots.append(jnp.where((lane1 > o + r) & (lane1 < o + 8), 0.0, q))
            if r < 7:
                c = jnp.where(sub > r, col[r], 0.0)
                f = c * inv
                for j in range(r + 1, 8):
                    col[j] = col[j] - f * above[r, j]
                head = jnp.where((lane == o + r) & (sub > r), 0.0, head) - c * q
        rows[kb] = head
        inside = (lane >= o) & (lane < o + 8)
        for i in range(kb + 1, 16):
            c = [jnp.broadcast_to(rows[i][:, o + j : o + j + 1], (8, 128)) for j in range(8)]
            x = jnp.where(inside, 0.0, rows[i])
            for r in range(8):
                f = c[r] * inverses[r]
                for j in range(r + 1, 8):
                    c[j] = c[j] - f * above[r, j]
                x = x - c[r] * pivots[r]
            rows[i] = x
    full = jnp.concatenate(rows, axis=0)
    r = lax.broadcasted_iota(jnp.int32, (128, 128), 0)
    c = lax.broadcasted_iota(jnp.int32, (128, 128), 1)
    d = jnp.sum(jnp.where(r == c, full, 0.0), axis=1, keepdims=True)
    return jnp.where(r > c, full, jnp.where(r == c, 1.0, 0.0)) * lax.rsqrt(d)


def kernel(
    a_hbm, t_hbm, out_ref,
    a, t, part1, core1, got1, acc1, last1, hi1, sketch, left, proj, projx, projf, right,
    part3, core3, got3, acc3, last3, hi3,
    gram1, gx1, gs1, full1, gram2, gx2, gs2, full2, factor1, factor2,
    load_sem, entered, s_core1, r_core1, s_one1, r_one1, s_two1, r_two1, s_hi1, r_hi1,
    s_core3, r_core3, s_one3, r_one3, s_two3, r_two3, s_hi3, r_hi3,
    s_g1, r_g1, s_z1, r_z1, s_b1, r_b1,
    s_g2, r_g2, s_z2, r_z2, s_b2, r_b2,
    s_ag, r_ag, s_fw, r_fw, s_p, r_p, s_pf, r_pf,
):
    zl = lax.axis_index("rows")
    ci = lax.axis_index("cols")
    zh, x, y, k = ci // 32, (ci // 8) % 4, (ci // 2) % 4, ci % 2

    def block(body):
        pl.when(zl >= 0)(body)

    def at(zl_, zh_, x_, y_, k_):
        return (zl_, ((zh_ * 4 + x_) * 4 + y_) * 2 + k_)

    other_core = at(zl, zh, x, y, 1 - k)
    other_hi = at(zl, 1 - zh, x, y, k)

    def plane_peer(o):
        return (x + o[0]) % 4, (y + o[1]) % 4

    def plane_dev(o):
        px, py = plane_peer(o)
        return at(zl, zh, px, py, k)

    def remote(src, dst, ss, rs, dev):
        return pltpu.make_async_remote_copy(
            src_ref=src, dst_ref=dst, send_sem=ss, recv_sem=rs, device_id=dev, device_id_type=MESH
        )

    column = [(dz, dk) for dz in (4, 3, 5, 2, 6, 1, 7, 0) for dk in (0, 1) if dz or dk]

    nearby = [(dz, dk) for dz in (2, 3, 1, 0) for dk in (0, 1) if dz or dk]

    def nearby_dev(dz, dk):
        return at((zl + dz) % 4, zh, x, y, (k + dk) % 2)

    def column_dev(dz, dk):
        z = (zh * 4 + zl + dz) % 8
        return at(z % 4, z // 4, x, y, (k + dk) % 2)

    load_t = pltpu.make_async_copy(t_hbm, t, load_sem.at[8])
    load_t.start()
    loads = []
    order = (2, 1, 3, 0)
    for n, dx in enumerate(order):
        px = (x + dx) % 4
        for h in range(2):
            ref = pl.ds(pl.multiple_of(h * 2048 + px * 512, 512), 512)
            copy = pltpu.make_async_copy(a_hbm.at[ref, :], a.at[ref, :], load_sem.at[2 * n + h])
            copy.start()
            loads.append(copy)

    def x_dev(d):
        return at(zl, zh, (x + d) % 4, y, k)

    def y_dev(d):
        return at(zl, zh, x, (y + d) % 4, k)

    def z_dev(d):
        z = (zh * 4 + zl + d) % 8
        return at(z % 4, z // 4, x, y, k)

    barrier = pltpu.get_barrier_semaphore()
    entry = [other_core] + [f(d) for d in (2, 1, 3) for f in (x_dev, y_dev)]
    within = [z_dev(d) for d in (2, 6, 1, 7)]
    for device in within + entry:
        pl.semaphore_signal(barrier, inc=1, device_id=device, device_id_type=MESH)

    top, low = pl.ds(0, 32), pl.ds(32, 32)
    around = (2, 1, 3)

    def reduce_columns(weights, part, core, got, acc, last, s_core, r_core, s_one, r_one, s_two, r_two, first, after):
        cores, ones = {}, []

        def exchange(n, dx):
            px = (x + dx) % 4
            cores[dx] = remote(
                part.at[:, px, :, 1 - k], core.at[px], s_core.at[n], r_core.at[n], other_core
            )
            cores[dx].start()

        def add_and_send(dx):
            px = (x + dx) % 4
            cores[dx].wait_recv()
            for py in range(4):
                part[:, px, py, k] = part[:, px, py, k] + core[px, :, py]
            if dx:
                copy = remote(
                    part.at[:, px, :, k, top], got.at[0, dx - 1], s_one.at[0, dx - 1], r_one.at[0, dx - 1], x_dev(dx)
                )
                copy.start()
                ones.append(copy)
            for d in around:
                remote(
                    part.at[:, px, (y + d) % 4, k, low], got.at[1, d - 1, :, px], s_one.at[1, d - 1],
                    r_one.at[1, d - 1], y_dev(d),
                ).start()

        for n, dx in enumerate(order):
            px = (x + dx) % 4
            for h in range(2):
                if first:
                    loads[2 * n + h].wait()

                @block
                def _(h=h, px=px):
                    ref = pl.ds(pl.multiple_of(h * 2048 + px * 512, 512), 512)
                    piece = jnp.dot(a[ref, :], weights[...], preferred_element_type=F32)
                    part[h, px] = piece.reshape(4, 2, 64, 128)

            if first and n == 0:
                continue
            if first and n == 1:
                pl.semaphore_wait(barrier, len(entry) + len(within))
                exchange(0, order[0])
            exchange(n, dx)
            after(n)
            if n:
                add_and_send(order[n - 1])
        add_and_send(order[-1])
        after(4)
        for d in around:
            ones.append(
                remote(
                    part.at[:, :, (y + d) % 4, k, low], got.at[1, d - 1], s_one.at[1, d - 1], r_one.at[1, d - 1], y_dev(d)
                )
            )
        for copy in ones[:3]:
            copy.wait_recv()
        for i in range(4):
            acc[0, i] = part[:, x, i, k, top] + (got[0, 0, :, i] + got[0, 1, :, i]) + got[0, 2, :, i]
        twos = []
        for d in around:
            copy = remote(
                acc.at[0, (y + d) % 4], last.at[0, d - 1], s_two.at[0, d - 1], r_two.at[0, d - 1], y_dev(d)
            )
            copy.start()
            twos.append(copy)
        for copy in ones[3:]:
            copy.wait_recv()
        for i in range(4):
            acc[1, i] = part[:, i, y, k, low] + (got[1, 0, :, i] + got[1, 1, :, i]) + got[1, 2, :, i]
        for d in around:
            copy = remote(
                acc.at[1, (x + d) % 4], last.at[1, d - 1], s_two.at[1, d - 1], r_two.at[1, d - 1], x_dev(d)
            )
            copy.start()
            twos.append(copy)
        for copy in twos:
            copy.wait_recv()
        return (
            acc[0, y] + (last[0, 0] + last[0, 1]) + last[0, 2],
            acc[1, x] + (last[1, 0] + last[1, 1]) + last[1, 2],
            list(cores.values()) + ones + twos,
        )

    def all_reduce(gram, gx, gs, full, s_g, r_g, s_z, r_z, s_b, r_b, group, group_dev, group_slot):
        sends = []
        mine = x * 4 + y
        for s, o in enumerate(PLANE):
            px, py = plane_peer(o)
            copy = remote(gram.at[px * 4 + py], gx.at[s], s_g.at[s], r_g.at[s], plane_dev(o))
            copy.start()
            sends.append(copy)
        yield
        total = gram[mine]
        for s in range(15):
            sends[s].wait_recv()
            total = total + gx[s]
        slot = group_slot(0, 0)
        gs[slot] = total
        for s, o in enumerate(group):
            copy = remote(gs.at[slot], gs.at[slot], s_z.at[s], r_z.at[s], group_dev(*o))
            copy.start()
            sends.append(copy)
        yield
        for copy in sends[15:]:
            copy.wait_recv()
        total = gs[0]
        for s in range(1, len(group) + 1):
            total = total + gs[s]
        full[mine] = total
        casts = []
        for s, o in enumerate(PLANE):
            copy = remote(full.at[mine], full.at[mine], s_b.at[s], r_b.at[s], plane_dev(o))
            copy.start()
            casts.append(copy)
        yield
        for copy in casts:
            copy.wait_recv()
        for copy in sends + casts:
            copy.wait_send()
        yield

    load_t.wait()
    def enter(n):
        if n == 1:
            for device in within:
                pl.semaphore_signal(entered.at[0], inc=1, device_id=device, device_id_type=MESH)

    upper, lower, pending1 = reduce_columns(
        t, part1, core1, got1, acc1, last1, s_core1, r_core1, s_one1, r_one1, s_two1, r_two1, True, enter
    )
    pl.semaphore_wait(entered.at[0], len(within))
    pl.semaphore_signal(entered.at[1], inc=1, device_id=other_core, device_id_type=MESH)
    hi1[0, :, top] = upper
    hi1[0, :, low] = lower
    swap = remote(hi1.at[0], hi1.at[1], s_hi1, r_hi1, other_hi)
    swap.start()
    pl.semaphore_wait(entered.at[1], 1)
    swap.wait_recv()
    sketch[:, x, y, k] = hi1[0] + hi1[1]

    spread = [[], []]
    for half, rows, devs in ((0, top, y_dev), (1, low, x_dev)):
        for d in around:
            mine = sketch.at[:, x, y, k, rows]
            copy = remote(mine, mine, s_ag.at[half, 0, d - 1], r_ag.at[half, 0, d - 1], devs(d))
            copy.start()
            spread[half].append(copy)
    rows = (hi1[0] + hi1[1]).reshape(128, 128)
    gram1[...] = lax.dot_general(
        rows, rows, (((0,), (0,)), ((), ())), precision=HIGH, preferred_element_type=F32
    ).reshape(16, 8, 128)
    reduction = all_reduce(
        gram1, gx1, gs1, full1, s_g1, r_g1, s_z1, r_z1, s_b1, r_b1, nearby, nearby_dev,
        lambda dz, dk: ((zl + dz) % 4) * 2 + (k + dk) % 2,
    )
    next(reduction)
    forward = {}

    def strip(half, d):
        if half:
            return sketch.at[:, :, (y + d) % 4, k, low]
        return sketch.at[:, (x + d) % 4, :, k, top]

    def to_core(half, d):
        forward[half, d] = remote(
            strip(half, d), strip(half, d), s_fw.at[half, d], r_fw.at[half, d], other_core
        )
        forward[half, d].start()

    for half, devs in ((0, x_dev), (1, y_dev)):
        for copy in spread[half]:
            copy.wait_recv()
        for d in around:
            mine = strip(half, 0)
            copy = remote(mine, mine, s_ag.at[half, 1, d - 1], r_ag.at[half, 1, d - 1], devs(d))
            copy.start()
            spread[half].append(copy)
        to_core(half, 0)

    def pass_on(d):
        for half in range(2):
            spread[half][3 + around.index(d)].wait_recv()
            to_core(half, (4 - d) % 4)

    next(reduction)
    next(reduction)
    pass_on(1)
    pass_on(3)
    pass_on(2)
    next(reduction)

    @block
    def _():
        factor1[...] = inverse_factor(full1[...].reshape(128, 128))

    gram = full1[...].reshape(128, 128)
    diag = lax.broadcasted_iota(jnp.int32, (128, 128), 0) == lax.broadcasted_iota(jnp.int32, (128, 128), 1)
    scale = lax.rsqrt(jnp.sum(jnp.where(diag, gram, 0.0), keepdims=True) / 128)

    for copy in forward.values():
        copy.wait_recv()

    for h in range(2):
        for px in range(4):
            piece = lax.dot_general(
                factor1[...], sketch[h, px].reshape(512, 128), (((1,), (1,)), ((), ())),
                precision=HIGH, preferred_element_type=F32,
            )
            left[:, h * 2048 + px * 512 : h * 2048 + px * 512 + 512] = piece.astype(BF16)

    gives = []
    for n, dz in enumerate((2, 1, 3, 0)):
        pz = (zl + dz) % 4

        @block
        def _(pz=pz):
            ref = pl.ds(pl.multiple_of(pz * 256, 256), 256)
            proj[pz] = jnp.dot(left[...], a[:, ref], preferred_element_type=F32)

        if dz:
            copy = remote(proj.at[pz], projx.at[n], s_p.at[n], r_p.at[n], at(pz, zh, x, y, k))
            copy.start()
            gives.append(copy)
    total = proj[zl]
    for n in range(3):
        gives[n].wait_recv()
        total = total + projx[n]
    total = total * scale
    projf[zl] = total.astype(BF16)
    shares = []
    for n, dz in enumerate((2, 1, 3)):
        copy = remote(
            projf.at[zl], projf.at[zl], s_pf.at[n], r_pf.at[n], at((zl + dz) % 4, zh, x, y, k)
        )
        copy.start()
        shares.append(copy)
    gram2[...] = lax.dot_general(
        total, total, (((1,), (1,)), ((), ())), precision=HIGH, preferred_element_type=F32
    ).reshape(16, 8, 128)
    reduction = all_reduce(
        gram2, gx2, gs2, full2, s_g2, r_g2, s_z2, r_z2, s_b2, r_b2, column, column_dev,
        lambda dz, dk: ((zh * 4 + zl + dz) % 8) * 2 + (k + dk) % 2,
    )
    next(reduction)
    for copy in shares:
        copy.wait_recv()

    for pz in range(4):
        right[pz * 256 : pz * 256 + 256, :] = projf[pz].T

    def step(n):
        if n in (0, 4):
            next(reduction)

    upper, lower, pending3 = reduce_columns(
        right, part3, core3, got3, acc3, last3, s_core3, r_core3, s_one3, r_one3, s_two3, r_two3, False, step
    )
    hi3[0, :, top] = upper
    hi3[0, :, low] = lower
    swap3 = remote(hi3.at[0, 1 - zh], hi3.at[1, 0], s_hi3, r_hi3, other_hi)
    swap3.start()
    next(reduction)

    @block
    def _():
        factor2[...] = inverse_factor(full2[...].reshape(128, 128))

    swap3.wait_recv()
    out_ref[...] = lax.dot_general(
        hi3[0, zh] + hi3[1, 0], factor2[...], (((1,), (1,)), ((), ())),
        precision=HIGH, preferred_element_type=F32,
    )
    for copy in pending1 + [swap] + spread[0] + spread[1] + list(forward.values()) + gives + shares + pending3 + [swap3]:
        copy.wait_send()


def local(responses, test_matrix):
    v = pltpu.VMEM
    dma = pltpu.SemaphoreType.DMA
    scratch = [
        v((4096, 1024), BF16), v((1024, 128), BF16),
        v((2, 4, 4, 2, 64, 128), F32), v((4, 2, 4, 64, 128), F32), v((2, 3, 2, 4, 32, 128), F32), v((2, 4, 2, 32, 128), F32), v((2, 3, 2, 32, 128), F32), v((2, 2, 64, 128), F32),
        v((2, 4, 4, 2, 64, 128), F32), v((128, 4096), BF16),
        v((4, 128, 256), F32), v((3, 128, 256), F32), v((4, 128, 256), BF16), v((1024, 128), BF16),
        v((2, 4, 4, 2, 64, 128), F32), v((4, 2, 4, 64, 128), F32), v((2, 3, 2, 4, 32, 128), F32), v((2, 4, 2, 32, 128), F32), v((2, 3, 2, 32, 128), F32), v((2, 2, 64, 128), F32),
        v((16, 8, 128), F32), v((15, 8, 128), F32), v((8, 8, 128), F32), v((16, 8, 128), F32),
        v((16, 8, 128), F32), v((15, 8, 128), F32), v((16, 8, 128), F32), v((16, 8, 128), F32),
        v((128, 128), F32), v((128, 128), F32),
        dma((9,)), pltpu.SemaphoreType.REGULAR((2,)),
    ]
    scratch += [dma((4,)), dma((4,)), dma((2, 3)), dma((2, 3)), dma((2, 3)), dma((2, 3)), dma, dma] * 2
    scratch += [dma((15,)), dma((15,)), dma((7,)), dma((7,)), dma((15,)), dma((15,))]
    scratch += [dma((15,)), dma((15,)), dma((15,)), dma((15,)), dma((15,)), dma((15,))]
    scratch += [dma((2, 2, 3)), dma((2, 2, 3)), dma((2, 4)), dma((2, 4)), dma((3,)), dma((3,)), dma((3,)), dma((3,))]
    return pl.pallas_call(
        kernel,
        out_shape=jax.ShapeDtypeStruct((64, 128), F32),
        in_specs=[pl.BlockSpec(memory_space=pltpu.HBM)] * 2,
        out_specs=pl.BlockSpec(memory_space=pltpu.VMEM),
        scratch_shapes=scratch,
        compiler_params=pltpu.CompilerParams(
            collective_id=0, has_side_effects=True, vmem_limit_bytes=64 * 2**20 - 2**17
        ),
        name="power_iteration",
    )(responses, test_matrix)


def solution(mesh):
    in_specs = (P("rows", "cols"), P("cols", None))
    out_specs = P(("rows", "cols"), None)
    return jax.shard_map(local, mesh=mesh, in_specs=in_specs, out_specs=out_specs, check_vma=False)
```

```python
import functools

import jax
import jax.numpy as jnp
from jax import lax
from jax.experimental import pallas as pl
from jax.experimental.pallas import tpu as pltpu
from jax.sharding import PartitionSpec as P

F32 = jnp.float32
BF16 = jnp.bfloat16
MESH = pl.DeviceIdType.MESH
HIGH = lax.Precision.HIGHEST

PLANE = sorted(
    [(i, j) for i in range(4) for j in range(4) if i or j],
    key=lambda o: -(min(o[0], 4 - o[0]) + min(o[1], 4 - o[1])),
)


def eliminate(full, first, last):
    lane = lax.broadcasted_iota(jnp.int32, (8, 128), 1)
    sub = lax.broadcasted_iota(jnp.int32, (8, 128), 0)
    lane1 = lane[:1]
    rows = [full[8 * i : 8 * i + 8] for i in range(16)]
    for kb in range(first, last):
        o = 8 * kb
        head = rows[kb]
        col = [jnp.broadcast_to(head[:, o + j : o + j + 1], (8, 128)) for j in range(8)]
        inverses, pivots, above = [], [], {}
        for r in range(8):
            inv = 1.0 / col[r][r : r + 1]
            inverses.append(inv)
            for j in range(r + 1, 8):
                above[r, j] = col[j][r : r + 1]
            q = jnp.where(lane1 == o + r, 1.0, head[r : r + 1]) * inv
            pivots.append(jnp.where((lane1 > o + r) & (lane1 < o + 8), 0.0, q))
            if r < 7:
                c = jnp.where(sub > r, col[r], 0.0)
                f = c * inv
                for j in range(r + 1, 8):
                    col[j] = col[j] - f * above[r, j]
                head = jnp.where((lane == o + r) & (sub > r), 0.0, head) - c * q
        rows[kb] = head
        inside = (lane >= o) & (lane < o + 8)
        for i in range(kb + 1, 16):
            c = [jnp.broadcast_to(rows[i][:, o + j : o + j + 1], (8, 128)) for j in range(8)]
            x = jnp.where(inside, 0.0, rows[i])
            for r in range(8):
                f = c[r] * inverses[r]
                for j in range(r + 1, 8):
                    c[j] = c[j] - f * above[r, j]
                x = x - c[r] * pivots[r]
            rows[i] = x
    return jnp.concatenate(rows, axis=0)


def inverse_rows(full, first, last):
    r = lax.broadcasted_iota(jnp.int32, (last - first, 128), 0) + first
    c = lax.broadcasted_iota(jnp.int32, (last - first, 128), 1)
    full = full[first:last]
    d = jnp.sum(jnp.where(r == c, full, 0.0), axis=1, keepdims=True)
    return jnp.where(r > c, full, jnp.where(r == c, 1.0, 0.0)) * lax.rsqrt(d)


def kernel(
    a_hbm, t_hbm, out_ref,
    a, t, part1, core1, got1, acc1, last1, hi1, sketch, left, proj, projx, projf, right,
    part3, core3, got3, acc3, last3, hi3,
    gram1, gx1, gs1, full1, gram2, gx2, gs2, full2, factor1, rows1, factor2,
    load_sem, entered, s_core1, r_core1, s_one1, r_one1, s_two1, r_two1, s_hi1, r_hi1,
    s_core3, r_core3, s_one3, r_one3, s_two3, r_two3, s_hi3, r_hi3,
    s_g1, r_g1, s_z1, r_z1, s_b1, r_b1,
    s_g2, r_g2, s_z2, r_z2, s_b2, r_b2,
    s_ag, r_ag, s_fw, r_fw, s_p, r_p, s_pf, r_pf,
):
    zl = lax.axis_index("rows")
    ci = lax.axis_index("cols")
    zh, x, y, k = ci // 32, (ci // 8) % 4, (ci // 2) % 4, ci % 2

    def block(body):
        pl.when(zl >= 0)(body)

    def at(zl_, zh_, x_, y_, k_):
        return (zl_, ((zh_ * 4 + x_) * 4 + y_) * 2 + k_)

    other_core = at(zl, zh, x, y, 1 - k)
    other_hi = at(zl, 1 - zh, x, y, k)

    def plane_peer(o):
        return (x + o[0]) % 4, (y + o[1]) % 4

    def plane_dev(o):
        px, py = plane_peer(o)
        return at(zl, zh, px, py, k)

    def remote(src, dst, ss, rs, dev):
        return pltpu.make_async_remote_copy(
            src_ref=src, dst_ref=dst, send_sem=ss, recv_sem=rs, device_id=dev, device_id_type=MESH
        )

    column = [(dz, dk) for dz in (4, 3, 5, 2, 6, 1, 7, 0) for dk in (0, 1) if dz or dk]

    nearby = [(dz, dk) for dz in (2, 3, 1, 0) for dk in (0, 1) if dz or dk]

    def nearby_dev(dz, dk):
        return at((zl + dz) % 4, zh, x, y, (k + dk) % 2)

    def column_dev(dz, dk):
        z = (zh * 4 + zl + dz) % 8
        return at(z % 4, z // 4, x, y, (k + dk) % 2)

    load_t = pltpu.make_async_copy(t_hbm, t, load_sem.at[8])
    load_t.start()
    loads = []
    order = (2, 1, 3, 0)
    for n, dx in enumerate(order):
        px = (x + dx) % 4
        for h in range(2):
            ref = pl.ds(pl.multiple_of(h * 2048 + px * 512, 512), 512)
            copy = pltpu.make_async_copy(a_hbm.at[ref, :], a.at[ref, :], load_sem.at[2 * n + h])
            copy.start()
            loads.append(copy)

    def x_dev(d):
        return at(zl, zh, (x + d) % 4, y, k)

    def y_dev(d):
        return at(zl, zh, x, (y + d) % 4, k)

    def z_dev(d):
        z = (zh * 4 + zl + d) % 8
        return at(z % 4, z // 4, x, y, k)

    barrier = pltpu.get_barrier_semaphore()
    entry = [other_core] + [f(d) for d in (2, 1, 3) for f in (x_dev, y_dev)]
    within = [z_dev(d) for d in (2, 6, 1, 7)]
    for device in within + entry:
        pl.semaphore_signal(barrier, inc=1, device_id=device, device_id_type=MESH)

    top, low = pl.ds(0, 32), pl.ds(32, 32)
    around = (2, 1, 3)

    def reduce_columns(weights, part, core, got, acc, last, s_core, r_core, s_one, r_one, s_two, r_two, first, after):
        cores, ones = {}, []

        def exchange(n, dx):
            px = (x + dx) % 4
            cores[dx] = remote(
                part.at[:, px, :, 1 - k], core.at[px], s_core.at[n], r_core.at[n], other_core
            )
            cores[dx].start()

        def add_and_send(dx):
            px = (x + dx) % 4
            cores[dx].wait_recv()
            for py in range(4):
                part[:, px, py, k] = part[:, px, py, k] + core[px, :, py]
            if dx:
                copy = remote(
                    part.at[:, px, :, k, top], got.at[0, dx - 1], s_one.at[0, dx - 1], r_one.at[0, dx - 1], x_dev(dx)
                )
                copy.start()
                ones.append(copy)
            for d in around:
                remote(
                    part.at[:, px, (y + d) % 4, k, low], got.at[1, d - 1, :, px], s_one.at[1, d - 1],
                    r_one.at[1, d - 1], y_dev(d),
                ).start()

        for n, dx in enumerate(order):
            px = (x + dx) % 4
            for h in range(2):
                if first:
                    loads[2 * n + h].wait()

                @block
                def _(h=h, px=px):
                    ref = pl.ds(pl.multiple_of(h * 2048 + px * 512, 512), 512)
                    piece = jnp.dot(a[ref, :], weights[...], preferred_element_type=F32)
                    part[h, px] = piece.reshape(4, 2, 64, 128)

            if first and n == 0:
                continue
            if first and n == 1:
                pl.semaphore_wait(barrier, len(entry) + len(within))
                exchange(0, order[0])
            exchange(n, dx)
            after(n)
            if n:
                add_and_send(order[n - 1])
        add_and_send(order[-1])
        after(4)
        for d in around:
            ones.append(
                remote(
                    part.at[:, :, (y + d) % 4, k, low], got.at[1, d - 1], s_one.at[1, d - 1], r_one.at[1, d - 1], y_dev(d)
                )
            )
        for copy in ones[:3]:
            copy.wait_recv()
        for i in range(4):
            acc[0, i] = part[:, x, i, k, top] + (got[0, 0, :, i] + got[0, 1, :, i]) + got[0, 2, :, i]
        twos = []
        for d in around:
            copy = remote(
                acc.at[0, (y + d) % 4], last.at[0, d - 1], s_two.at[0, d - 1], r_two.at[0, d - 1], y_dev(d)
            )
            copy.start()
            twos.append(copy)
        for copy in ones[3:]:
            copy.wait_recv()
        for i in range(4):
            acc[1, i] = part[:, i, y, k, low] + (got[1, 0, :, i] + got[1, 1, :, i]) + got[1, 2, :, i]
        for d in around:
            copy = remote(
                acc.at[1, (x + d) % 4], last.at[1, d - 1], s_two.at[1, d - 1], r_two.at[1, d - 1], x_dev(d)
            )
            copy.start()
            twos.append(copy)
        after(5)
        for copy in twos:
            copy.wait_recv()
        return (
            acc[0, y] + (last[0, 0] + last[0, 1]) + last[0, 2],
            acc[1, x] + (last[1, 0] + last[1, 1]) + last[1, 2],
            list(cores.values()) + ones + twos,
        )

    def all_reduce(gram, gx, gs, full, s_g, r_g, s_z, r_z, s_b, r_b, group, group_dev, group_slot):
        sends = []
        mine = x * 4 + y
        for s, o in enumerate(PLANE):
            px, py = plane_peer(o)
            copy = remote(gram.at[px * 4 + py], gx.at[s], s_g.at[s], r_g.at[s], plane_dev(o))
            copy.start()
            sends.append(copy)
        yield
        total = gram[mine]
        for s in range(15):
            sends[s].wait_recv()
            total = total + gx[s]
        slot = group_slot(0, 0)
        gs[slot] = total
        for s, o in enumerate(group):
            copy = remote(gs.at[slot], gs.at[slot], s_z.at[s], r_z.at[s], group_dev(*o))
            copy.start()
            sends.append(copy)
        yield
        for copy in sends[15:]:
            copy.wait_recv()
        total = gs[0]
        for s in range(1, len(group) + 1):
            total = total + gs[s]
        full[mine] = total
        casts = []
        for s, o in enumerate(PLANE):
            copy = remote(full.at[mine], full.at[mine], s_b.at[s], r_b.at[s], plane_dev(o))
            copy.start()
            casts.append(copy)
        yield
        for copy in casts:
            copy.wait_recv()
        for copy in sends + casts:
            copy.wait_send()
        yield

    load_t.wait()
    def enter(n):
        if n == 1:
            for device in within:
                pl.semaphore_signal(entered.at[0], inc=1, device_id=device, device_id_type=MESH)

    upper, lower, pending1 = reduce_columns(
        t, part1, core1, got1, acc1, last1, s_core1, r_core1, s_one1, r_one1, s_two1, r_two1, True, enter
    )
    pl.semaphore_wait(entered.at[0], len(within))
    pl.semaphore_signal(entered.at[1], inc=1, device_id=other_core, device_id_type=MESH)
    hi1[0, :, top] = upper
    hi1[0, :, low] = lower
    swap = remote(hi1.at[0], hi1.at[1], s_hi1, r_hi1, other_hi)
    swap.start()
    pl.semaphore_wait(entered.at[1], 1)
    swap.wait_recv()
    sketch[:, x, y, k] = hi1[0] + hi1[1]

    spread = [[], []]
    for half, rows, devs in ((0, top, y_dev), (1, low, x_dev)):
        for d in around:
            mine = sketch.at[:, x, y, k, rows]
            copy = remote(mine, mine, s_ag.at[half, 0, d - 1], r_ag.at[half, 0, d - 1], devs(d))
            copy.start()
            spread[half].append(copy)
    rows = (hi1[0] + hi1[1]).reshape(128, 128)
    gram1[...] = lax.dot_general(
        rows, rows, (((0,), (0,)), ((), ())), precision=HIGH, preferred_element_type=F32
    ).reshape(16, 8, 128)
    reduction = all_reduce(
        gram1, gx1, gs1, full1, s_g1, r_g1, s_z1, r_z1, s_b1, r_b1, nearby, nearby_dev,
        lambda dz, dk: ((zl + dz) % 4) * 2 + (k + dk) % 2,
    )
    next(reduction)
    forward = {}

    def strip(half, d):
        if half:
            return sketch.at[:, :, (y + d) % 4, k, low]
        return sketch.at[:, (x + d) % 4, :, k, top]

    def to_core(half, d):
        forward[half, d] = remote(
            strip(half, d), strip(half, d), s_fw.at[half, d], r_fw.at[half, d], other_core
        )
        forward[half, d].start()

    for half, devs in ((0, x_dev), (1, y_dev)):
        for copy in spread[half]:
            copy.wait_recv()
        for d in around:
            mine = strip(half, 0)
            copy = remote(mine, mine, s_ag.at[half, 1, d - 1], r_ag.at[half, 1, d - 1], devs(d))
            copy.start()
            spread[half].append(copy)
        to_core(half, 0)

    def pass_on(d):
        for half in range(2):
            spread[half][3 + around.index(d)].wait_recv()
            to_core(half, (4 - d) % 4)

    next(reduction)
    next(reduction)
    pass_on(1)
    pass_on(3)
    pass_on(2)
    next(reduction)

    gram = full1[...].reshape(128, 128)
    diag = lax.broadcasted_iota(jnp.int32, (128, 128), 0) == lax.broadcasted_iota(jnp.int32, (128, 128), 1)
    scale = lax.rsqrt(jnp.sum(jnp.where(diag, gram, 0.0), keepdims=True) / 128)

    gives = []
    for half in range(2):
        span = pl.ds(64 * half, 64)

        @block
        def _(half=half, span=span):
            full = eliminate(factor1[...] if half else full1[...].reshape(128, 128), 8 * half, 8 * half + 8)
            if not half:
                factor1[...] = full
            rows1[...] = inverse_rows(full, 64 * half, 64 * half + 64)

        if not half:
            for copy in forward.values():
                copy.wait_recv()

        @block
        def _(span=span):
            for h in range(2):
                for px in range(4):
                    piece = lax.dot_general(
                        rows1[...], sketch[h, px].reshape(512, 128), (((1,), (1,)), ((), ())),
                        precision=HIGH, preferred_element_type=F32,
                    )
                    left[span, h * 2048 + px * 512 : h * 2048 + px * 512 + 512] = piece.astype(BF16)

        for n, dz in enumerate((2, 1, 3, 0)):
            pz = (zl + dz) % 4

            @block
            def _(pz=pz, span=span):
                ref = pl.ds(pl.multiple_of(pz * 256, 256), 256)
                proj[pz, span] = jnp.dot(left[span, :], a[:, ref], preferred_element_type=F32)

            if dz:
                copy = remote(
                    proj.at[pz, span], projx.at[n, span], s_p.at[half, n], r_p.at[half, n], at(pz, zh, x, y, k)
                )
                copy.start()
                gives.append(copy)
    for copy in gives:
        copy.wait_recv()
    total = proj[zl] + projx[0] + projx[1] + projx[2]
    total = total * scale
    projf[zl] = total.astype(BF16)
    shares = []
    for n, dz in enumerate((2, 1, 3)):
        copy = remote(
            projf.at[zl], projf.at[zl], s_pf.at[n], r_pf.at[n], at((zl + dz) % 4, zh, x, y, k)
        )
        copy.start()
        shares.append(copy)
    gram2[...] = lax.dot_general(
        total, total, (((1,), (1,)), ((), ())), precision=HIGH, preferred_element_type=F32
    ).reshape(16, 8, 128)
    reduction = all_reduce(
        gram2, gx2, gs2, full2, s_g2, r_g2, s_z2, r_z2, s_b2, r_b2, column, column_dev,
        lambda dz, dk: ((zh * 4 + zl + dz) % 8) * 2 + (k + dk) % 2,
    )
    next(reduction)
    for copy in shares:
        copy.wait_recv()

    for pz in range(4):
        right[pz * 256 : pz * 256 + 256, :] = projf[pz].T

    def step(n):
        if n in (0, 4):
            next(reduction)
    upper, lower, pending3 = reduce_columns(
        right, part3, core3, got3, acc3, last3, s_core3, r_core3, s_one3, r_one3, s_two3, r_two3, False, step
    )
    hi3[0, :, top] = upper
    hi3[0, :, low] = lower
    swap3 = remote(hi3.at[0, 1 - zh], hi3.at[1, 0], s_hi3, r_hi3, other_hi)
    swap3.start()
    next(reduction)

    @block
    def _():
        full = eliminate(full2[...].reshape(128, 128), 0, 16)
        factor2[...] = inverse_rows(full, 0, 128)

    swap3.wait_recv()
    out_ref[...] = lax.dot_general(
        hi3[0, zh] + hi3[1, 0], factor2[...], (((1,), (1,)), ((), ())),
        precision=HIGH, preferred_element_type=F32,
    )
    for copy in pending1 + [swap] + spread[0] + spread[1] + list(forward.values()) + gives + shares + pending3 + [swap3]:
        copy.wait_send()


def local(responses, test_matrix):
    v = pltpu.VMEM
    dma = pltpu.SemaphoreType.DMA
    scratch = [
        v((4096, 1024), BF16), v((1024, 128), BF16),
        v((2, 4, 4, 2, 64, 128), F32), v((4, 2, 4, 64, 128), F32), v((2, 3, 2, 4, 32, 128), F32), v((2, 4, 2, 32, 128), F32), v((2, 3, 2, 32, 128), F32), v((2, 2, 64, 128), F32),
        v((2, 4, 4, 2, 64, 128), F32), v((128, 4096), BF16),
        v((4, 128, 256), F32), v((3, 128, 256), F32), v((4, 128, 256), BF16), v((1024, 128), BF16),
        v((2, 4, 4, 2, 64, 128), F32), v((4, 2, 4, 64, 128), F32), v((2, 3, 2, 4, 32, 128), F32), v((2, 4, 2, 32, 128), F32), v((2, 3, 2, 32, 128), F32), v((2, 2, 64, 128), F32),
        v((16, 8, 128), F32), v((15, 8, 128), F32), v((8, 8, 128), F32), v((16, 8, 128), F32),
        v((16, 8, 128), F32), v((15, 8, 128), F32), v((16, 8, 128), F32), v((16, 8, 128), F32),
        v((128, 128), F32), v((64, 128), F32), v((128, 128), F32),
        dma((9,)), pltpu.SemaphoreType.REGULAR((2,)),
    ]
    scratch += [dma((4,)), dma((4,)), dma((2, 3)), dma((2, 3)), dma((2, 3)), dma((2, 3)), dma, dma] * 2
    scratch += [dma((15,)), dma((15,)), dma((7,)), dma((7,)), dma((15,)), dma((15,))]
    scratch += [dma((15,)), dma((15,)), dma((15,)), dma((15,)), dma((15,)), dma((15,))]
    scratch += [dma((2, 2, 3)), dma((2, 2, 3)), dma((2, 4)), dma((2, 4)), dma((2, 3)), dma((2, 3)), dma((3,)), dma((3,))]
    return pl.pallas_call(
        kernel,
        out_shape=jax.ShapeDtypeStruct((64, 128), F32),
        in_specs=[pl.BlockSpec(memory_space=pltpu.HBM)] * 2,
        out_specs=pl.BlockSpec(memory_space=pltpu.VMEM),
        scratch_shapes=scratch,
        compiler_params=pltpu.CompilerParams(
            collective_id=0, has_side_effects=True, vmem_limit_bytes=64 * 2**20 - 2**17
        ),
        name="power_iteration",
    )(responses, test_matrix)


def solution(mesh):
    in_specs = (P("rows", "cols"), P("cols", None))
    out_specs = P(("rows", "cols"), None)
    return jax.shard_map(local, mesh=mesh, in_specs=in_specs, out_specs=out_specs, check_vma=False)
```

```python
import functools

import jax
import jax.numpy as jnp
from jax import lax
from jax.experimental import pallas as pl
from jax.experimental.pallas import tpu as pltpu
from jax.sharding import PartitionSpec as P

F32 = jnp.float32
BF16 = jnp.bfloat16
MESH = pl.DeviceIdType.MESH
HIGH = lax.Precision.HIGHEST

PLANE = sorted(
    [(i, j) for i in range(4) for j in range(4) if i or j],
    key=lambda o: -(min(o[0], 4 - o[0]) + min(o[1], 4 - o[1])),
)


def eliminate(full, first, last):
    lane = lax.broadcasted_iota(jnp.int32, (8, 128), 1)
    sub = lax.broadcasted_iota(jnp.int32, (8, 128), 0)
    lane1 = lane[:1]
    rows = [full[8 * i : 8 * i + 8] for i in range(16)]
    for kb in range(first, last):
        o = 8 * kb
        head = rows[kb]
        col = [jnp.broadcast_to(head[:, o + j : o + j + 1], (8, 128)) for j in range(8)]
        inverses, pivots, above = [], [], {}
        for r in range(8):
            inv = 1.0 / col[r][r : r + 1]
            inverses.append(inv)
            for j in range(r + 1, 8):
                above[r, j] = col[j][r : r + 1]
            q = jnp.where(lane1 == o + r, 1.0, head[r : r + 1]) * inv
            pivots.append(jnp.where((lane1 > o + r) & (lane1 < o + 8), 0.0, q))
            if r < 7:
                c = jnp.where(sub > r, col[r], 0.0)
                f = c * inv
                for j in range(r + 1, 8):
                    col[j] = col[j] - f * above[r, j]
                head = jnp.where((lane == o + r) & (sub > r), 0.0, head) - c * q
        rows[kb] = head
        inside = (lane >= o) & (lane < o + 8)
        for i in range(kb + 1, 16):
            c = [jnp.broadcast_to(rows[i][:, o + j : o + j + 1], (8, 128)) for j in range(8)]
            x = jnp.where(inside, 0.0, rows[i])
            for r in range(8):
                f = c[r] * inverses[r]
                for j in range(r + 1, 8):
                    c[j] = c[j] - f * above[r, j]
                x = x - c[r] * pivots[r]
            rows[i] = x
    return jnp.concatenate(rows, axis=0)


def inverse_rows(full, first, last):
    r = lax.broadcasted_iota(jnp.int32, (last - first, 128), 0) + first
    c = lax.broadcasted_iota(jnp.int32, (last - first, 128), 1)
    full = full[first:last]
    d = jnp.sum(jnp.where(r == c, full, 0.0), axis=1, keepdims=True)
    return jnp.where(r > c, full, jnp.where(r == c, 1.0, 0.0)) * lax.rsqrt(d)


def kernel(
    a_hbm, t_hbm, out_ref,
    a, t, part1, core1, got1, acc1, last1, hi1, sketch, left, proj, projx, projf, right,
    part3, core3, got3, acc3, last3, hi3,
    gram1, gx1, gs1, full1, gram2, gx2, gs2, full2, factor1, rows1, factor2,
    load_sem, entered, s_core1, r_core1, s_one1, r_one1, s_two1, r_two1, s_hi1, r_hi1,
    s_core3, r_core3, s_one3, r_one3, s_two3, r_two3, s_hi3, r_hi3,
    s_g1, r_g1, s_z1, r_z1, s_b1, r_b1,
    s_g2, r_g2, s_z2, r_z2, s_b2, r_b2,
    s_ag, r_ag, s_fw, r_fw, s_p, r_p, s_pf, r_pf,
):
    zl = lax.axis_index("rows")
    ci = lax.axis_index("cols")
    zh, x, y, k = ci // 32, (ci // 8) % 4, (ci // 2) % 4, ci % 2

    def block(body):
        pl.when(zl >= 0)(body)

    def at(zl_, zh_, x_, y_, k_):
        return (zl_, ((zh_ * 4 + x_) * 4 + y_) * 2 + k_)

    other_core = at(zl, zh, x, y, 1 - k)
    other_hi = at(zl, 1 - zh, x, y, k)

    def plane_peer(o):
        return (x + o[0]) % 4, (y + o[1]) % 4

    def plane_dev(o):
        px, py = plane_peer(o)
        return at(zl, zh, px, py, k)

    def remote(src, dst, ss, rs, dev):
        return pltpu.make_async_remote_copy(
            src_ref=src, dst_ref=dst, send_sem=ss, recv_sem=rs, device_id=dev, device_id_type=MESH
        )

    column = [(dz, dk) for dz in (4, 3, 5, 2, 6, 1, 7, 0) for dk in (0, 1) if dz or dk]

    nearby = [(dz, dk) for dz in (2, 3, 1, 0) for dk in (0, 1) if dz or dk]

    def nearby_dev(dz, dk):
        return at((zl + dz) % 4, zh, x, y, (k + dk) % 2)

    def column_dev(dz, dk):
        z = (zh * 4 + zl + dz) % 8
        return at(z % 4, z // 4, x, y, (k + dk) % 2)

    load_t = pltpu.make_async_copy(t_hbm, t, load_sem.at[8])
    load_t.start()
    loads = []
    order = (2, 1, 3, 0)
    for n, dx in enumerate(order):
        px = (x + dx) % 4
        for h in range(2):
            ref = pl.ds(pl.multiple_of(h * 2048 + px * 512, 512), 512)
            copy = pltpu.make_async_copy(a_hbm.at[ref, :], a.at[ref, :], load_sem.at[2 * n + h])
            copy.start()
            loads.append(copy)

    def x_dev(d):
        return at(zl, zh, (x + d) % 4, y, k)

    def y_dev(d):
        return at(zl, zh, x, (y + d) % 4, k)

    def z_dev(d):
        z = (zh * 4 + zl + d) % 8
        return at(z % 4, z // 4, x, y, k)

    barrier = pltpu.get_barrier_semaphore()
    entry = [other_core] + [f(d) for d in (2, 1, 3) for f in (x_dev, y_dev)]
    within = [z_dev(d) for d in (2, 6, 1, 7)]
    for device in within + entry:
        pl.semaphore_signal(barrier, inc=1, device_id=device, device_id_type=MESH)

    top, low = pl.ds(0, 32), pl.ds(32, 32)
    around = (2, 1, 3)

    def reduce_columns(weights, part, core, got, acc, last, s_core, r_core, s_one, r_one, s_two, r_two, first, after, done):
        cores, ones = {}, []

        def exchange(n, dx):
            px = (x + dx) % 4
            cores[dx] = remote(
                part.at[:, px, :, 1 - k], core.at[px], s_core.at[n], r_core.at[n], other_core
            )
            cores[dx].start()

        def add_and_send(dx):
            px = (x + dx) % 4
            cores[dx].wait_recv()
            for py in range(4):
                part[:, px, py, k] = part[:, px, py, k] + core[px, :, py]
            if dx:
                copy = remote(
                    part.at[:, px, :, k, top], got.at[0, dx - 1], s_one.at[0, dx - 1], r_one.at[0, dx - 1], x_dev(dx)
                )
                copy.start()
                ones.append(copy)
            for d in around:
                remote(
                    part.at[:, px, (y + d) % 4, k, low], got.at[1, d - 1, :, px], s_one.at[1, d - 1],
                    r_one.at[1, d - 1], y_dev(d),
                ).start()

        for n, dx in enumerate(order):
            px = (x + dx) % 4
            for h in range(2):
                if first:
                    loads[2 * n + h].wait()

                @block
                def _(h=h, px=px):
                    ref = pl.ds(pl.multiple_of(h * 2048 + px * 512, 512), 512)
                    piece = jnp.dot(a[ref, :], weights[...], preferred_element_type=F32)
                    part[h, px] = piece.reshape(4, 2, 64, 128)

            if first and n == 0:
                continue
            if first and n == 1:
                pl.semaphore_wait(barrier, len(entry) + len(within))
                exchange(0, order[0])
            exchange(n, dx)
            after(n)
            if n:
                add_and_send(order[n - 1])
        add_and_send(order[-1])
        after(4)
        for d in around:
            ones.append(
                remote(
                    part.at[:, :, (y + d) % 4, k, low], got.at[1, d - 1], s_one.at[1, d - 1], r_one.at[1, d - 1], y_dev(d)
                )
            )
        for copy in ones[:3]:
            copy.wait_recv()
        for i in range(4):
            acc[0, i] = part[:, x, i, k, top] + (got[0, 0, :, i] + got[0, 1, :, i]) + got[0, 2, :, i]
        twos = []
        for d in around:
            copy = remote(
                acc.at[0, (y + d) % 4], last.at[0, d - 1], s_two.at[0, d - 1], r_two.at[0, d - 1], y_dev(d)
            )
            copy.start()
            twos.append(copy)
        for copy in ones[3:]:
            copy.wait_recv()
        for i in range(4):
            acc[1, i] = part[:, i, y, k, low] + (got[1, 0, :, i] + got[1, 1, :, i]) + got[1, 2, :, i]
        for d in around:
            copy = remote(
                acc.at[1, (x + d) % 4], last.at[1, d - 1], s_two.at[1, d - 1], r_two.at[1, d - 1], x_dev(d)
            )
            copy.start()
            twos.append(copy)
        after(5)
        for half, own in ((0, y), (1, x)):
            for copy in twos[3 * half : 3 * half + 3]:
                copy.wait_recv()
            done(half, acc[half, own] + (last[half, 0] + last[half, 1]) + last[half, 2])
        return list(cores.values()) + ones + twos

    def all_reduce(gram, gx, gs, full, s_g, r_g, s_z, r_z, s_b, r_b, group, group_dev, group_slot):
        sends = []
        mine = x * 4 + y
        for s, o in enumerate(PLANE):
            px, py = plane_peer(o)
            copy = remote(gram.at[px * 4 + py], gx.at[s], s_g.at[s], r_g.at[s], plane_dev(o))
            copy.start()
            sends.append(copy)
        yield
        total = gram[mine]
        for s in range(15):
            sends[s].wait_recv()
            total = total + gx[s]
        slot = group_slot(0, 0)
        gs[slot] = total
        for s, o in enumerate(group):
            copy = remote(gs.at[slot], gs.at[slot], s_z.at[s], r_z.at[s], group_dev(*o))
            copy.start()
            sends.append(copy)
        yield
        for copy in sends[15:]:
            copy.wait_recv()
        total = gs[0]
        for s in range(1, len(group) + 1):
            total = total + gs[s]
        full[mine] = total
        casts = []
        for s, o in enumerate(PLANE):
            copy = remote(full.at[mine], full.at[mine], s_b.at[s], r_b.at[s], plane_dev(o))
            copy.start()
            casts.append(copy)
        yield
        for copy in casts:
            copy.wait_recv()
        for copy in sends + casts:
            copy.wait_send()
        yield

    load_t.wait()
    def enter(n):
        if n == 1:
            for device in within:
                pl.semaphore_signal(entered.at[0], inc=1, device_id=device, device_id_type=MESH)

    swaps = []

    def swap_hi(half, value):
        if not half:
            pl.semaphore_wait(entered.at[0], len(within))
            pl.semaphore_signal(entered.at[1], inc=1, device_id=other_core, device_id_type=MESH)
        rows = low if half else top
        hi1[0, :, rows] = value
        copy = remote(hi1.at[0, :, rows], hi1.at[1, :, rows], s_hi1.at[half], r_hi1.at[half], other_hi)
        copy.start()
        swaps.append(copy)

    pending1 = reduce_columns(
        t, part1, core1, got1, acc1, last1, s_core1, r_core1, s_one1, r_one1, s_two1, r_two1, True, enter, swap_hi
    )
    pl.semaphore_wait(entered.at[1], 1)

    spread = [[], []]
    for half, rows, devs in ((0, top, y_dev), (1, low, x_dev)):
        swaps[half].wait_recv()
        sketch[:, x, y, k, rows] = hi1[0, :, rows] + hi1[1, :, rows]
        for d in around:
            mine = sketch.at[:, x, y, k, rows]
            copy = remote(mine, mine, s_ag.at[half, 0, d - 1], r_ag.at[half, 0, d - 1], devs(d))
            copy.start()
            spread[half].append(copy)
    rows = (hi1[0] + hi1[1]).reshape(128, 128)
    gram1[...] = lax.dot_general(
        rows, rows, (((0,), (0,)), ((), ())), precision=HIGH, preferred_element_type=F32
    ).reshape(16, 8, 128)
    reduction = all_reduce(
        gram1, gx1, gs1, full1, s_g1, r_g1, s_z1, r_z1, s_b1, r_b1, nearby, nearby_dev,
        lambda dz, dk: ((zl + dz) % 4) * 2 + (k + dk) % 2,
    )
    next(reduction)
    forward = {}

    def strip(half, d):
        if half:
            return sketch.at[:, :, (y + d) % 4, k, low]
        return sketch.at[:, (x + d) % 4, :, k, top]

    def to_core(half, d):
        forward[half, d] = remote(
            strip(half, d), strip(half, d), s_fw.at[half, d], r_fw.at[half, d], other_core
        )
        forward[half, d].start()

    for half, devs in ((0, x_dev), (1, y_dev)):
        for copy in spread[half]:
            copy.wait_recv()
        for d in around:
            mine = strip(half, 0)
            copy = remote(mine, mine, s_ag.at[half, 1, d - 1], r_ag.at[half, 1, d - 1], devs(d))
            copy.start()
            spread[half].append(copy)
        to_core(half, 0)

    def pass_on(d):
        for half in range(2):
            spread[half][3 + around.index(d)].wait_recv()
            to_core(half, (4 - d) % 4)

    next(reduction)
    next(reduction)
    pass_on(1)
    pass_on(3)
    pass_on(2)
    next(reduction)

    gram = full1[...].reshape(128, 128)
    diag = lax.broadcasted_iota(jnp.int32, (128, 128), 0) == lax.broadcasted_iota(jnp.int32, (128, 128), 1)
    scale = lax.rsqrt(jnp.sum(jnp.where(diag, gram, 0.0), keepdims=True) / 128)

    gives = []
    for half in range(2):
        span = pl.ds(64 * half, 64)

        @block
        def _(half=half, span=span):
            full = eliminate(factor1[...] if half else full1[...].reshape(128, 128), 8 * half, 8 * half + 8)
            if not half:
                factor1[...] = full
            rows1[...] = inverse_rows(full, 64 * half, 64 * half + 64)

        if not half:
            for copy in forward.values():
                copy.wait_recv()

        @block
        def _(span=span):
            for h in range(2):
                for px in range(4):
                    piece = lax.dot_general(
                        rows1[...], sketch[h, px].reshape(512, 128), (((1,), (1,)), ((), ())),
                        precision=HIGH, preferred_element_type=F32,
                    )
                    left[span, h * 2048 + px * 512 : h * 2048 + px * 512 + 512] = piece.astype(BF16)

        for n, dz in enumerate((2, 1, 3, 0)):
            pz = (zl + dz) % 4

            @block
            def _(pz=pz, span=span):
                ref = pl.ds(pl.multiple_of(pz * 256, 256), 256)
                proj[pz, span] = jnp.dot(left[span, :], a[:, ref], preferred_element_type=F32)

            if dz:
                copy = remote(
                    proj.at[pz, span], projx.at[n, span], s_p.at[half, n], r_p.at[half, n], at(pz, zh, x, y, k)
                )
                copy.start()
                gives.append(copy)
    for copy in gives:
        copy.wait_recv()
    total = proj[zl] + projx[0] + projx[1] + projx[2]
    total = total * scale
    projf[zl] = total.astype(BF16)
    shares = []
    for n, dz in enumerate((2, 1, 3)):
        copy = remote(
            projf.at[zl], projf.at[zl], s_pf.at[n], r_pf.at[n], at((zl + dz) % 4, zh, x, y, k)
        )
        copy.start()
        shares.append(copy)
    gram2[...] = lax.dot_general(
        total, total, (((1,), (1,)), ((), ())), precision=HIGH, preferred_element_type=F32
    ).reshape(16, 8, 128)
    reduction = all_reduce(
        gram2, gx2, gs2, full2, s_g2, r_g2, s_z2, r_z2, s_b2, r_b2, column, column_dev,
        lambda dz, dk: ((zh * 4 + zl + dz) % 8) * 2 + (k + dk) % 2,
    )
    next(reduction)

    def turn(pz):
        @block
        def _():
            right[pl.ds(pl.multiple_of(pz * 256, 256), 256), :] = projf[pz].T

    turn(zl)
    for n in (1, 2, 0):
        shares[n].wait_recv()
        turn((zl + 4 - (2, 1, 3)[n]) % 4)

    def step(n):
        if n in (0, 4):
            next(reduction)
    def swap_last(half, value):
        rows = low if half else top
        hi3[0, :, rows] = value
        copy = remote(
            hi3.at[0, 1 - zh, rows], hi3.at[1, 0, rows], s_hi3.at[half], r_hi3.at[half], other_hi
        )
        copy.start()
        swaps.append(copy)

    pending3 = reduce_columns(
        right, part3, core3, got3, acc3, last3, s_core3, r_core3, s_one3, r_one3, s_two3, r_two3, False, step, swap_last
    )
    next(reduction)

    @block
    def _():
        full = eliminate(full2[...].reshape(128, 128), 0, 16)
        factor2[...] = inverse_rows(full, 0, 128)

    for copy in swaps[2:]:
        copy.wait_recv()
    out_ref[...] = lax.dot_general(
        hi3[0, zh] + hi3[1, 0], factor2[...], (((1,), (1,)), ((), ())),
        precision=HIGH, preferred_element_type=F32,
    )
    for copy in pending1 + swaps + spread[0] + spread[1] + list(forward.values()) + gives + shares + pending3:
        copy.wait_send()


def local(responses, test_matrix):
    v = pltpu.VMEM
    dma = pltpu.SemaphoreType.DMA
    scratch = [
        v((4096, 1024), BF16), v((1024, 128), BF16),
        v((2, 4, 4, 2, 64, 128), F32), v((4, 2, 4, 64, 128), F32), v((2, 3, 2, 4, 32, 128), F32), v((2, 4, 2, 32, 128), F32), v((2, 3, 2, 32, 128), F32), v((2, 2, 64, 128), F32),
        v((2, 4, 4, 2, 64, 128), F32), v((128, 4096), BF16),
        v((4, 128, 256), F32), v((3, 128, 256), F32), v((4, 128, 256), BF16), v((1024, 128), BF16),
        v((2, 4, 4, 2, 64, 128), F32), v((4, 2, 4, 64, 128), F32), v((2, 3, 2, 4, 32, 128), F32), v((2, 4, 2, 32, 128), F32), v((2, 3, 2, 32, 128), F32), v((2, 2, 64, 128), F32),
        v((16, 8, 128), F32), v((15, 8, 128), F32), v((8, 8, 128), F32), v((16, 8, 128), F32),
        v((16, 8, 128), F32), v((15, 8, 128), F32), v((16, 8, 128), F32), v((16, 8, 128), F32),
        v((128, 128), F32), v((64, 128), F32), v((128, 128), F32),
        dma((9,)), pltpu.SemaphoreType.REGULAR((2,)),
    ]
    scratch += [dma((4,)), dma((4,)), dma((2, 3)), dma((2, 3)), dma((2, 3)), dma((2, 3)), dma((2,)), dma((2,))] * 2
    scratch += [dma((15,)), dma((15,)), dma((7,)), dma((7,)), dma((15,)), dma((15,))]
    scratch += [dma((15,)), dma((15,)), dma((15,)), dma((15,)), dma((15,)), dma((15,))]
    scratch += [dma((2, 2, 3)), dma((2, 2, 3)), dma((2, 4)), dma((2, 4)), dma((2, 3)), dma((2, 3)), dma((3,)), dma((3,))]
    return pl.pallas_call(
        kernel,
        out_shape=jax.ShapeDtypeStruct((64, 128), F32),
        in_specs=[pl.BlockSpec(memory_space=pltpu.HBM)] * 2,
        out_specs=pl.BlockSpec(memory_space=pltpu.VMEM),
        scratch_shapes=scratch,
        compiler_params=pltpu.CompilerParams(
            collective_id=0, has_side_effects=True, vmem_limit_bytes=64 * 2**20 - 2**17
        ),
        name="power_iteration",
    )(responses, test_matrix)


def solution(mesh):
    in_specs = (P("rows", "cols"), P("cols", None))
    out_specs = P(("rows", "cols"), None)
    return jax.shard_map(local, mesh=mesh, in_specs=in_specs, out_specs=out_specs, check_vma=False)
```
